256 devices in a mesh: dp: 32 (over y, z_hi, x), context: 8 (over z_lo, core).
Axes of the slice: x: 4, y: 4, z: 8 (z_hi: 2, z_lo: 4; z = z_hi * 4 + z_lo), core: 2. Of those that a mesh axis runs over, the one named last changes fastest.
Arguments:
- projected: bfloat16 [3, 16384, 4096], P(None, 'context', 'dp'), may hold values from -6 to 6
- filter_taps: bfloat16 [16384, 4096], P('context', 'dp'), may hold values from -0.046875 to 0.046875
- out_grad: bfloat16 [16384, 4096], P('context', 'dp'), may hold values from -6 to 6
- out_weight: bfloat16 [4096, 4096], P('dp', 'context'), may hold values from -0.09375 to 0.09375
Outputs:
- grad_streams: bfloat16 [3, 16384, 4096], P(None, 'context', 'dp')
- grad_filter: float32 [16384, 4096], P('context', 'dp')
- grad_weight: float32 [4096, 4096], P('dp', 'context')
The draws below stay inside these ranges and needn't reach their ends.
All inputs are finite; a program needn't handle non-finite values.
Results may differ from the reference program's by a relative error of at most 0.017.
Values may be sent and summed in bfloat16 or wider, within the bound.
A program may use at most 128 MiB of HBM per device.

```python
import math
import jax
import jax.numpy as jnp
from jax import lax

C = 4096
DW = 4096
BLOCK = 1024
TOK_DEV = 2048
LENGTH = 16384
N_CONTEXT = 8


def block_levels(stream_key, shape, shards, low, top_value):
    def one(position, blocks):
        heights = jax.random.uniform(jax.random.fold_in(jax.random.fold_in(stream_key, 6), position), (blocks,), jnp.float32, low / len(shards), top_value / len(shards))
        return jnp.repeat(jnp.exp(heights), shape[position] // blocks).reshape((-1,) + (1,) * (len(shape) - position - 1))

    factor_of = one(*shards[0])
    for cut in shards[1:]:
        factor_of = factor_of * one(*cut)
    return factor_of


def normal_values(stream_key, shape, spread, reach, shards=(), kind=jnp.bfloat16):
    array = spread * jax.random.normal(stream_key, shape, jnp.float32)
    if shards:
        array = array * block_levels(stream_key, shape, shards, -0.22, 0.18)
    return jnp.clip(array, -reach, reach).astype(kind)


def setup_inputs(seed: int = 0) -> dict:
    streams_of = jax.random.split(jax.random.key(seed), 5)
    return {
        "projected": normal_values(streams_of[0], (3, LENGTH, C), 1.0, 6.0, ((1, 8), (2, 32))),
        "filter_taps": normal_values(streams_of[1], (LENGTH, C), (1.0 / LENGTH ** 0.5), 0.046875, ((0, 8), (1, 32))),
        "out_grad": normal_values(streams_of[2], (LENGTH, DW), 1.0, 6.0, ((0, 8), (1, 32))),
        "out_weight": normal_values(streams_of[3], (C, DW), DW ** -0.5, 0.09375, ((0, 32), (1, 8))),
    }


def angles(leading, trailing, modulus):
    product = leading[:, None] * trailing[None, :] % modulus
    return 2.0 * math.pi / modulus * product.astype(jnp.float32)

def small_table(count_q, sign):
    steps_q = jnp.arange(count_q, dtype=jnp.int32)
    phases = angles(steps_q, steps_q, count_q)
    cosine = jnp.cos(phases)
    sines = sign * jnp.sin(phases)
    upper = jnp.stack([cosine, sines], 1)
    lower = jnp.stack([-sines, cosine], 1)
    return jnp.stack([upper, lower], 0).astype(jnp.bfloat16)

def forward_spectrum(signal):
    batches, length_all, channels = signal.shape
    half_block = BLOCK // 2
    count_q = length_all // half_block
    total_len = BLOCK * count_q
    blocks = signal.reshape(batches, half_block, count_q, channels)
    phases = angles(jnp.arange(BLOCK, dtype=jnp.int32), jnp.arange(half_block, dtype=jnp.int32), BLOCK)
    section_table = jnp.concatenate([jnp.cos(phases), -jnp.sin(phases)], 0).astype(jnp.bfloat16)
    partial_sum = jnp.einsum('kp,bpqc->bkqc', section_table.astype(jnp.float32), blocks.astype(jnp.float32), precision=lax.Precision.HIGHEST)
    real_part = partial_sum[:, :BLOCK]
    imag_part = partial_sum[:, BLOCK:]
    twist = angles(jnp.arange(BLOCK, dtype=jnp.int32), jnp.arange(count_q, dtype=jnp.int32), total_len)
    cosine = jnp.cos(twist)[:, :, None]
    sines = jnp.sin(twist)[:, :, None]
    turned = jnp.stack([real_part * cosine + imag_part * sines, imag_part * cosine - real_part * sines], 1).astype(jnp.bfloat16)
    table_q = small_table(count_q, 1.0)
    spectrum = jnp.einsum('okiq,bipqc->bopkc', table_q.astype(jnp.float32), turned.astype(jnp.float32), precision=lax.Precision.HIGHEST)
    return spectrum.astype(jnp.bfloat16)

def inverse_spectrum(spectrum):
    batches = spectrum.shape[0]
    count_q = spectrum.shape[3]
    channels = spectrum.shape[4]
    half_block = BLOCK // 2
    total_len = BLOCK * count_q
    table_q = small_table(count_q, -1.0)
    partial_sum = jnp.einsum('oqik,bipkc->bopqc', table_q.astype(jnp.float32), spectrum.astype(jnp.float32), precision=lax.Precision.HIGHEST)
    twist = angles(jnp.arange(BLOCK, dtype=jnp.int32), jnp.arange(count_q, dtype=jnp.int32), total_len)
    cosine = jnp.cos(twist)[:, :, None]
    sines = jnp.sin(twist)[:, :, None]
    real_part = partial_sum[:, 0]
    imag_part = partial_sum[:, 1]
    turned = jnp.stack([real_part * cosine - imag_part * sines, imag_part * cosine + real_part * sines], 1).astype(jnp.bfloat16)
    phases = angles(jnp.arange(half_block, dtype=jnp.int32), jnp.arange(BLOCK, dtype=jnp.int32), BLOCK)
    section_table = jnp.concatenate([jnp.cos(phases), -jnp.sin(phases)], 1).astype(jnp.bfloat16)
    merged = turned.reshape(batches, 2 * BLOCK, count_q, channels)
    values = jnp.einsum('pk,bkqc->bpqc', section_table.astype(jnp.float32), merged.astype(jnp.float32), precision=lax.Precision.HIGHEST)
    values = (values * (1.0 / total_len)).astype(jnp.bfloat16)
    return values.reshape(batches, half_block * count_q, channels)

def complex_product(first_spec, second_spec, conjugate):
    first_real = first_spec[:, 0].astype(jnp.float32)
    first_imag = first_spec[:, 1].astype(jnp.float32)
    second_real = second_spec[:, 0].astype(jnp.float32)
    second_imag = second_spec[:, 1].astype(jnp.float32)
    if conjugate:
        real_part = first_real * second_real + first_imag * second_imag
        imag_part = first_real * second_imag - first_imag * second_real
    else:
        real_part = first_real * second_real - first_imag * second_imag
        imag_part = first_real * second_imag + first_imag * second_real
    return jnp.stack([real_part, imag_part], 1).astype(jnp.bfloat16)

def reference(projected, filter_taps, out_grad, out_weight):
    length_all = projected.shape[1]
    loss_scale = 1.0 / math.sqrt(length_all)
    filter_spec = forward_spectrum(filter_taps[None])
    queries = projected[0].astype(jnp.float32)
    key_stream = projected[1].astype(jnp.float32)
    value_stream = projected[2].astype(jnp.float32)
    mixing = (key_stream * value_stream).astype(jnp.bfloat16)
    mixing_spec = forward_spectrum(mixing[None])
    conv = inverse_spectrum(complex_product(filter_spec, mixing_spec, False))[0]
    upstream = jnp.dot(out_grad, out_weight.T, preferred_element_type=jnp.float32)
    gated = (upstream * queries).astype(jnp.bfloat16)
    grad_spec = forward_spectrum(gated[None])
    grad_mixing = inverse_spectrum(complex_product(filter_spec, grad_spec, True))[0].astype(jnp.float32)
    grad_taps = inverse_spectrum(complex_product(mixing_spec, grad_spec, True))[0]
    conv_wide = conv.astype(jnp.float32)
    grad_streams = jnp.stack([upstream * conv_wide, grad_mixing * value_stream, grad_mixing * key_stream]).astype(jnp.bfloat16)
    output = (queries * conv_wide).astype(jnp.bfloat16)
    out_blocks = output.reshape(N_CONTEXT, TOK_DEV, output.shape[1])
    grad_blocks = out_grad.reshape(N_CONTEXT, TOK_DEV, out_grad.shape[1])

    def add_block(total, pair):
        term = loss_scale * jnp.dot(pair[0].T, pair[1], preferred_element_type=jnp.float32)
        term = lax.optimization_barrier(term.astype(jnp.bfloat16))
        return (total + term.astype(jnp.float32), None)
    start_total = jnp.zeros((output.shape[1], out_grad.shape[1]), jnp.float32)
    grad_weight, _ = lax.scan(add_block, start_total, (out_blocks, grad_blocks))
    grad_filter = loss_scale * grad_taps.astype(jnp.float32)
    return (grad_streams, grad_filter, grad_weight)
```

```python
import functools
import math

import jax
import jax.numpy as jnp
import ml_dtypes
import numpy as np
from jax import lax
from jax.experimental import pallas as pl
from jax.experimental.pallas import tpu as pltpu
from jax.sharding import PartitionSpec as P

CTX = 8
ROWS = 256
STEPS = 64
CH = 16
LEN = 16384
F32 = jnp.float32
BF = jnp.bfloat16
MESH = pl.DeviceIdType.MESH


def tables():
    s = np.arange(STEPS)
    klo = np.arange(STEPS) + 0.25
    th = 2 * np.pi * s[:, None] * klo[None, :] / STEPS
    eye = np.eye(CH)
    fwd = np.concatenate([np.kron(np.cos(th), eye), np.kron(-np.sin(th), eye)], 1)
    b = np.arange(ROWS)
    ph = 2 * np.pi * ((b[:, None] * b[None, :]) % ROWS) / ROWS
    c, sn = np.cos(ph), np.sin(ph)
    tf = np.block([[c, sn], [-sn, c]])
    ps = 2 * np.pi * b[:, None] * klo[None, :] / LEN
    twc = np.repeat(np.cos(ps), CH, axis=1).astype(np.float32)
    tws = np.repeat(np.sin(ps), CH, axis=1).astype(np.float32)
    perm = np.zeros((8, 8, CH, 8, 8, CH), np.float32)
    for a in range(8):
        for g in range(8):
            for k in range(CH):
                perm[a, g, k, g, a, k] = 1
    perm = perm.reshape(1024, 1024)
    low = lambda z: np.ascontiguousarray(z).astype(ml_dtypes.bfloat16)
    return low(perm), low(fwd), low(fwd.T), low(tf), low(tf.T), twc, tws


def kernel(
    proj, taps, grad, weight, perm_h, kf_h, ki_h, tf_h, ti_h, twc_h, tws_h,
    o_streams, o_filter, o_weight,
    qkv, tap, G, W, perm, kf, ki, tf, ti, twc, tws,
    cat, send, recv, spec, wide, up, conv, out_t,
    ps, ps2, pr1, pr2, outs, outf, outw,
    lsem, osem, gs, gr, xs, xr, ws, wr, rs, rr,
):
    me = lax.axis_index("dp")
    ctx = lax.axis_index("context")
    yy, hh, xx = me // 8, (me // 4) % 2, me % 4
    zz, core = ctx // 2, ctx % 2
    sib = ctx + 1 - 2 * core

    def dev(dy, dx, flip):
        h = (1 - hh) if flip else hh
        return (lax.rem(yy + dy + 4, 4) * 2 + h) * 4 + lax.rem(xx + dx + 4, 4)

    loads = {}

    def load(name, src, dst, k):
        loads[name] = pltpu.make_async_copy(src, dst, lsem.at[k])
        loads[name].start()

    load("g", grad, G.at[me], 0)
    load("w", weight, W.at[ctx], 1)
    load("qkv", proj, qkv, 2)
    load("perm", perm_h, perm, 3)
    load("tap", taps, tap, 4)
    load("kf", kf_h, kf, 5)
    load("tf", tf_h, tf, 6)
    load("twc", twc_h, twc, 7)
    load("tws", tws_h, tws, 8)
    load("ki", ki_h, ki, 9)
    load("ti", ti_h, ti, 10)

    bar = pltpu.get_barrier_semaphore()
    for r in range(1, CTX):
        pl.semaphore_signal(bar, inc=1, device_id=(me, lax.rem(ctx + r, CTX)), device_id_type=MESH)
    for d in (dev(0, 1, 0), dev(0, -1, 0), dev(1, 0, 0), dev(-1, 0, 0), dev(0, 0, 1)):
        pl.semaphore_signal(bar, inc=1, device_id=(d, ctx), device_id_type=MESH)
    pl.semaphore_wait(bar, CTX - 1 + 5)

    sent = []

    def remote(src, dst, ssem, rsem, where):
        copy = pltpu.make_async_remote_copy(
            src_ref=src, dst_ref=dst, send_sem=ssem, recv_sem=rsem,
            device_id=where, device_id_type=MESH,
        )
        copy.start()
        sent.append(copy)

    def arrived(buf, rsem):
        pltpu.make_async_remote_copy(
            src_ref=buf, dst_ref=buf, send_sem=gs.at[0], recv_sem=rsem,
            device_id=(me, sib), device_id_type=MESH,
        ).wait_recv()

    nsend = [0]

    def piece(i, lo, n):
        return G.at[i, pl.ds(lo * 512, n * 512)]

    def push(i, lo, n, to):
        k = nsend[0]
        nsend[0] += 1
        p = piece(i, lo, n)
        remote(p, p, gs.at[k], gr.at[i, lo], (to, ctx))

    def got(i, lo, n):
        arrived(piece(i, lo, n), gr.at[i, lo])

    def place(half, u, v, flip):
        return dev(v, u, flip) if half == 0 else dev(u, v, flip)

    def nb(half, axis, step):
        return place(half, step, 0, 0) if axis == 0 else place(half, 0, step, 0)

    def e0(flip):
        src = dev(0, 0, flip)
        for axis in (0, 1):
            for half in (0, 1):
                for step in (1, -1):
                    push(src, 2 * half, 2, nb(half, axis, step))

    def e1(flip):
        for half in (0, 1):
            for u in (-1, 1):
                got(place(half, u, 0, flip), 2 * half, 2)
                q = 2 * half + (0 if u == -1 else 1)
                push(place(half, u, 0, flip), q, 1, nb(half, 0, -u))
        for u in (-1, 1):
            for half in (0, 1):
                for step in (1, -1):
                    push(place(half, u, 0, flip), 2 * half, 2, nb(half, 1, step))

    def e2(flip):
        for q in (0, 1):
            for half in (0, 1):
                i = place(half, 2, 0, flip)
                got(i, 2 * half + q, 1)
                for step in (1, -1):
                    push(i, 2 * half + q, 1, nb(half, 1, step))

    def e3(flip, us):
        for u in us:
            for half in (0, 1):
                for v in (-1, 1):
                    i = place(half, u, v, flip)
                    if u == 2:
                        got(i, 2 * half, 1)
                        got(i, 2 * half + 1, 1)
                    else:
                        got(i, 2 * half, 2)
                    q = 2 * half + (0 if v == -1 else 1)
                    push(i, q, 1, nb(half, 1, -v))

    def e4(flip):
        for u in (0, -1, 1, 2):
            for half in (0, 1):
                i = place(half, u, 2, flip)
                got(i, 2 * half, 1)
                got(i, 2 * half + 1, 1)

    def exchange(sig):
        for r in range(1, CTX):
            to = lax.rem(ctx + r, CTX)
            remote(send.at[sig, to], recv.at[sig, ctx], xs.at[sig, r], xr.at[sig, r], (me, to))
        own = pltpu.make_async_copy(send.at[sig, ctx], recv.at[sig, ctx], xr.at[sig, 0])
        own.start()
        return own

    def exchanged(sig, own):
        own.wait()
        for r in range(1, CTX):
            frm = lax.rem(ctx - r + CTX, CTX)
            arrived(recv.at[sig, frm], xr.at[sig, r])

    def dot(a, b):
        return jnp.dot(a, b, preferred_element_type=F32)

    def chunk(n):
        return pl.ds(pl.multiple_of(n * 256, 256), 256)

    def spread(sig):
        def body(n, _):
            z = dot(cat[...], perm[:, chunk(n)]).astype(BF)
            send[sig, 2 * n] = z[:, :128]
            send[sig, 2 * n + 1] = z[:, 128:]
            return 0
        lax.fori_loop(0, 4, body, 0)

    def gathered(sig):
        for d in range(CTX):
            cat[:, d * 128:(d + 1) * 128] = recv[sig, d]

    def collect(sig, use):
        gathered(sig)

        def body(n, _):
            z = dot(cat[...], perm[:, chunk(n)])
            for k in (0, 1):
                use(pl.ds(pl.multiple_of((2 * n + k) * 256, 256), 256), z[:, k * 128:(k + 1) * 128])
            return 0
        lax.fori_loop(0, 4, body, 0)

    def forward(sig):
        gathered(sig)

        def body(n, _):
            lanes = chunk(n)
            x = cat[...]
            re = dot(x, kf[:, lanes])
            im = dot(x, kf[:, pl.ds(pl.multiple_of(1024 + n * 256, 256), 256)])
            c, s = twc[:, lanes], tws[:, lanes]
            y = jnp.concatenate([(re * c + im * s).astype(BF), (im * c - re * s).astype(BF)], 0)
            spec[sig, :, lanes] = dot(tf[...], y).astype(BF)
            return 0
        lax.fori_loop(0, 4, body, 0)

    def inverse(first, second, conj, sig):
        def body(n, _):
            lanes = chunk(n)
            ar = spec[first, 0:256, lanes].astype(F32)
            ai = spec[first, 256:512, lanes].astype(F32)
            br = spec[second, 0:256, lanes].astype(F32)
            bi = spec[second, 256:512, lanes].astype(F32)
            if conj:
                pr, pi = ar * br + ai * bi, ar * bi - ai * br
            else:
                pr, pi = ar * br - ai * bi, ar * bi + ai * br
            p = jnp.concatenate([pr.astype(BF), pi.astype(BF)], 0)
            v = dot(ti[...], p)
            vr, vi = v[:256], v[256:]
            c, s = twc[:, lanes], tws[:, lanes]
            wide[:, lanes] = (vr * c - vi * s).astype(BF)
            wide[:, pl.ds(pl.multiple_of(1024 + n * 256, 256), 256)] = (vi * c + vr * s).astype(BF)
            return 0
        lax.fori_loop(0, 4, body, 0)

        def last(n, _):
            z = (dot(wide[...], ki[:, chunk(n)]) * (1.0 / LEN)).astype(BF)
            send[sig, 2 * n] = z[:, :128]
            send[sig, 2 * n + 1] = z[:, 128:]
            return 0
        lax.fori_loop(0, 4, last, 0)

    def upstream(flip):
        h = (1 - hh) if flip else hh

        def body(t, _):
            rows = pl.ds(pl.multiple_of(t * 256, 256), 256)
            acc = up[rows, :] if flip else jnp.zeros((256, 128), F32)
            for y in range(4):
                g = y * 2 + h
                x = jnp.concatenate([G[4 * g + k, rows, :] for k in range(4)], 1)
                acc = acc + lax.dot_general(
                    x, W[g], (((1,), (1,)), ((), ())), preferred_element_type=F32
                )
            up[rows, :] = acc
            return 0
        lax.fori_loop(0, 8, body, 0)

    loads["g"].wait()
    e0(0)
    for half in (0, 1):
        push(me, 2 * half, 2, dev(0, 0, 1))
    loads["w"].wait()
    for r in range(1, 4):
        remote(W.at[ctx], W.at[ctx], ws.at[r], wr.at[r], (me, lax.rem(zz + r, 4) * 2 + core))
    remote(W.at[ctx], W.at[ctx], ws.at[4], wr.at[4], (me, sib))
    loads["qkv"].wait()
    loads["perm"].wait()
    for a in range(8):
        rows = slice(a * 256, (a + 1) * 256)
        cat[:, a * 128:(a + 1) * 128] = (qkv[1, rows].astype(F32) * qkv[2, rows].astype(F32)).astype(BF)
    spread(0)
    own0 = exchange(0)
    loads["tap"].wait()
    for a in range(8):
        cat[:, a * 128:(a + 1) * 128] = tap[a * 256:(a + 1) * 256, :]
    spread(1)
    own1 = exchange(1)

    e1(0)
    e2(0)
    e3(0, (0, -1, 1, 2))

    for r in range(1, 4):
        frm = lax.rem(zz - r + 4, 4) * 2 + core
        arrived(W.at[frm], wr.at[r])
        remote(W.at[frm], W.at[frm], ws.at[4 + r], wr.at[4 + r], (me, sib))

    par = dev(0, 0, 1)
    for half in (0, 1):
        got(par, 2 * half, 2)
    e0(1)
    for k in ("kf", "tf", "twc", "tws"):
        loads[k].wait()
    exchanged(0, own0)
    forward(0)
    e1(1)
    exchanged(1, own1)
    forward(1)
    e2(1)
    loads["ki"].wait()
    loads["ti"].wait()
    inverse(1, 0, False, 3)
    own3 = exchange(3)
    e3(1, (0, -1))
    e4(0)
    arrived(W.at[sib], wr.at[4])
    for r in range(1, 4):
        arrived(W.at[lax.rem(zz - r + 4, 4) * 2 + 1 - core], wr.at[4 + r])
    upstream(0)
    e3(1, (1, 2))
    exchanged(3, own3)

    def use_conv(rows, z):
        conv[rows, :] = z.astype(BF)
    collect(3, use_conv)

    def turn(t, _):
        rows = pl.ds(pl.multiple_of(t * 256, 256), 256)
        o = (qkv[0, rows, :].astype(F32) * conv[rows, :].astype(F32)).astype(BF)
        out_t[:, rows] = o.T
        return 0
    lax.fori_loop(0, 8, turn, 0)
    e4(1)

    upstream(1)
    for a in range(8):
        rows = slice(a * 256, (a + 1) * 256)
        cat[:, a * 128:(a + 1) * 128] = (up[rows, :] * qkv[0, rows].astype(F32)).astype(BF)
    spread(2)
    own2 = exchange(2)

    def part(r, _):
        g = jnp.concatenate([G[4 * r + k] for k in range(4)], 1)
        ps[r] = (dot(out_t[...], g) * (1.0 / math.sqrt(LEN))).astype(BF)
        return 0
    lax.fori_loop(0, CTX, part, 0)
    for r in range(4):
        z = lax.rem(zz + r, 4)
        remote(ps.at[2 * z + 1 - core], pr1.at[r], rs.at[r], rr.at[r], (me, sib))
    for r in range(1, 4):
        z = lax.rem(zz + r, 4)
        arrived(pr1.at[r], rr.at[r])
        ps2[r] = (ps[2 * z + core].astype(F32) + pr1[r].astype(F32)).astype(BF)
        remote(ps2.at[r], pr2.at[r], rs.at[3 + r], rr.at[3 + r], (me, 2 * z + core))

    for a in range(8):
        rows = slice(a * 256, (a + 1) * 256)
        outs[0, rows, :] = (up[rows, :] * conv[rows, :].astype(F32)).astype(BF)
    writes = [pltpu.make_async_copy(outs.at[0], o_streams.at[0], osem.at[0])]
    writes[-1].start()

    exchanged(2, own2)
    forward(2)
    inverse(0, 2, True, 4)
    own4 = exchange(4)
    inverse(1, 2, True, 5)
    own5 = exchange(5)

    arrived(pr1.at[0], rr.at[0])
    total = ps[ctx].astype(F32) + pr1[0].astype(F32)
    for r in range(1, 4):
        arrived(pr2.at[r], rr.at[3 + r])
        total = total + pr2[r].astype(F32)
    outw[...] = total
    writes.append(pltpu.make_async_copy(outw, o_weight, osem.at[1]))
    writes[-1].start()

    exchanged(4, own4)

    def use_taps(rows, z):
        outf[rows, :] = z * (1.0 / math.sqrt(LEN))
    collect(4, use_taps)
    writes.append(pltpu.make_async_copy(outf, o_filter, osem.at[2]))
    writes[-1].start()

    exchanged(5, own5)

    def use_mix(rows, z):
        outs[1, rows, :] = (z * qkv[2, rows, :].astype(F32)).astype(BF)
        outs[2, rows, :] = (z * qkv[1, rows, :].astype(F32)).astype(BF)
    collect(5, use_mix)
    writes.append(pltpu.make_async_copy(outs.at[1], o_streams.at[1], osem.at[3]))
    writes[-1].start()
    writes.append(pltpu.make_async_copy(outs.at[2], o_streams.at[2], osem.at[4]))
    writes[-1].start()

    for copy in sent:
        copy.wait_send()
    for copy in writes:
        copy.wait()


def shards(projected, filter_taps, out_grad, out_weight):
    consts = [jnp.asarray(t) for t in tables()]
    vm = pltpu.VMEM
    sem = pltpu.SemaphoreType.DMA
    return pl.pallas_call(
        kernel,
        out_shape=(
            jax.ShapeDtypeStruct((3, 2048, 128), BF),
            jax.ShapeDtypeStruct((2048, 128), F32),
            jax.ShapeDtypeStruct((128, 512), F32),
        ),
        in_specs=[pl.BlockSpec(memory_space=pl.ANY)] * 11,
        out_specs=(pl.BlockSpec(memory_space=pl.ANY),) * 3,
        scratch_shapes=[
            vm((3, 2048, 128), BF),
            vm((2048, 128), BF),
            vm((32, 2048, 128), BF),
            vm((8, 128, 512), BF),
            vm((1024, 1024), BF),
            vm((1024, 2048), BF),
            vm((2048, 1024), BF),
            vm((512, 512), BF),
            vm((512, 512), BF),
            vm((256, 1024), F32),
            vm((256, 1024), F32),
            vm((256, 1024), BF),
            vm((6, 8, 256, 128), BF),
            vm((6, 8, 256, 128), BF),
            vm((3, 512, 1024), BF),
            vm((256, 2048), BF),
            vm((2048, 128), F32),
            vm((2048, 128), BF),
            vm((128, 2048), BF),
            vm((8, 128, 512), BF),
            vm((4, 128, 512), BF),
            vm((4, 128, 512), BF),
            vm((4, 128, 512), BF),
            vm((3, 2048, 128), BF),
            vm((2048, 128), F32),
            vm((128, 512), F32),
            sem((11,)), sem((5,)),
            sem((96,)), sem((32, 4)),
            sem((6, 8)), sem((6, 8)),
            sem((8,)), sem((8,)),
            sem((8,)), sem((8,)),
        ],
        compiler_params=pltpu.CompilerParams(
            collective_id=0, has_side_effects=True, vmem_limit_bytes=60 * 2**20
        ),
    )(projected, filter_taps, out_grad, out_weight, *consts)


def solution(mesh):
    placed = (P(None, "context", "dp"), P("context", "dp"), P("context", "dp"), P("dp", "context"))
    return jax.shard_map(
        shards,
        mesh=mesh,
        in_specs=placed,
        out_specs=(P(None, "context", "dp"), P("context", "dp"), P("dp", "context")),
        check_vma=False,
    )
```

```python
import functools
import math

import jax
import jax.numpy as jnp
import ml_dtypes
import numpy as np
from jax import lax
from jax.experimental import pallas as pl
from jax.experimental.pallas import tpu as pltpu
from jax.sharding import PartitionSpec as P

CTX = 8
ROWS = 256
STEPS = 64
CH = 16
LEN = 16384
F32 = jnp.float32
BF = jnp.bfloat16
MESH = pl.DeviceIdType.MESH
ALL = pl.ds(0, ROWS)
PASSES = ((0, 256), (0, 192), (192, 64))
PACE = 3


def tables():
    s = np.arange(STEPS)
    klo = np.arange(STEPS) + 0.25
    th = 2 * np.pi * s[:, None] * klo[None, :] / STEPS
    eye = np.eye(CH)
    fwd = np.concatenate([np.kron(np.cos(th), eye), np.kron(-np.sin(th), eye)], 1)
    b = np.arange(ROWS)
    ph = 2 * np.pi * ((b[:, None] * b[None, :]) % ROWS) / ROWS
    c, sn = np.cos(ph), np.sin(ph)
    tf = np.block([[c, sn], [-sn, c]])
    ps = 2 * np.pi * b[:, None] * klo[None, :] / LEN
    twc = np.repeat(np.cos(ps), CH, axis=1).astype(np.float32)
    tws = np.repeat(np.sin(ps), CH, axis=1).astype(np.float32)
    perm = np.zeros((8, 8, CH, 8, 8, CH), np.float32)
    for a in range(8):
        for g in range(8):
            for k in range(CH):
                perm[a, g, k, g, a, k] = 1
    perm = perm.reshape(1024, 1024)
    low = lambda z: np.ascontiguousarray(z).astype(ml_dtypes.bfloat16)
    return low(perm), low(fwd), low(fwd.T), low(tf), low(tf.T), twc, tws


def kernel(
    proj, taps, grad, weight, perm_h, kf_h, ki_h, tf_h, ti_h, twc_h, tws_h,
    o_streams, o_weight,
    qkv, tap, G, W, wt, perm, kf, ki, tf, ti, twc, tws,
    cat, send, recv, spec, turned, wide, up, conv, out_t,
    ps, psf, ps2, pr1, pr2, outs, outw,
    lsem, osem, gs, gr, xs, xr, ws, wr, rs, rr,
):
    me = lax.axis_index("dp")
    ctx = lax.axis_index("context")
    yy, hh, xx = me // 8, (me // 4) % 2, me % 4
    zz, core = ctx // 2, ctx % 2
    sib = ctx + 1 - 2 * core

    def dev(dy, dx, flip):
        h = (1 - hh) if flip else hh
        return (lax.rem(yy + dy + 4, 4) * 2 + h) * 4 + lax.rem(xx + dx + 4, 4)

    def chip(r):
        return lax.rem(zz + r + 4, 4)

    loads = {}

    def load(name, src, dst, k):
        loads[name] = pltpu.make_async_copy(src, dst, lsem.at[k])
        loads[name].start()

    load("g", grad, G.at[me], 0)
    load("qkv", proj, qkv, 2)
    load("perm", perm_h, perm, 3)
    load("tap", taps, tap, 4)
    load("w", weight, W.at[ctx], 1)
    load("kf", kf_h, kf, 5)
    load("tf", tf_h, tf, 6)
    load("twc", twc_h, twc, 7)
    load("tws", tws_h, tws, 8)
    load("ki", ki_h, ki, 9)
    load("ti", ti_h, ti, 10)

    bar = pltpu.get_barrier_semaphore()
    for r in range(1, CTX):
        pl.semaphore_signal(bar, inc=1, device_id=(me, lax.rem(ctx + r, CTX)), device_id_type=MESH)
    for d in (dev(0, 1, 0), dev(0, -1, 0), dev(1, 0, 0), dev(-1, 0, 0), dev(0, 0, 1)):
        pl.semaphore_signal(bar, inc=1, device_id=(d, ctx), device_id_type=MESH)
    pl.semaphore_wait(bar, CTX - 1 + 5)

    sent = []

    def remote(src, dst, ssem, rsem, where):
        copy = pltpu.make_async_remote_copy(
            src_ref=src, dst_ref=dst, send_sem=ssem, recv_sem=rsem,
            device_id=where, device_id_type=MESH,
        )
        copy.start()
        sent.append(copy)

    def arrived(buf, rsem):
        pltpu.make_async_remote_copy(
            src_ref=buf, dst_ref=buf, send_sem=gs.at[0], recv_sem=rsem,
            device_id=(me, sib), device_id_type=MESH,
        ).wait_recv()

    nsend = [0]
    todo = []

    def flush():
        while todo:
            todo.pop(0)()

    def piece(i, p, q, n):
        b0, nb = PASSES[p]
        return G.at[i, :, pl.ds(b0 + q * (nb // 4), n * (nb // 4)), :]

    def push(i, p, q, n, to):
        k = nsend[0]
        nsend[0] += 1
        r = piece(i, p, q, n)
        remote(r, r, gs.at[k], gr.at[i, 4 * (p // 2) + q], (to, ctx))
        if todo and k % PACE == PACE - 1:
            todo.pop(0)()

    def got(i, p, q, n):
        arrived(piece(i, p, q, n), gr.at[i, 4 * (p // 2) + q])

    def place(half, u, v, flip):
        return dev(v, u, flip) if half == 0 else dev(u, v, flip)

    def nb(half, axis, step):
        return place(half, step, 0, 0) if axis == 0 else place(half, 0, step, 0)

    def e0(p):
        flip = p > 0
        src = dev(0, 0, flip)
        for axis in (0, 1):
            for half in (0, 1):
                for step in (1, -1):
                    push(src, p, 2 * half, 2, nb(half, axis, step))

    def e1(p):
        flip = p > 0
        for half in (0, 1):
            for u in (-1, 1):
                i = place(half, u, 0, flip)
                got(i, p, 2 * half, 2)
                push(i, p, 2 * half + (0 if u == -1 else 1), 1, nb(half, 0, -u))
        for u in (-1, 1):
            for half in (0, 1):
                for step in (1, -1):
                    push(place(half, u, 0, flip), p, 2 * half, 2, nb(half, 1, step))

    def e2(p):
        flip = p > 0
        for q in (0, 1):
            for half in (0, 1):
                i = place(half, 2, 0, flip)
                got(i, p, 2 * half + q, 1)
                for step in (1, -1):
                    push(i, p, 2 * half + q, 1, nb(half, 1, step))

    def e3(p, us=(0, -1, 1, 2)):
        flip = p > 0
        for u in us:
            for half in (0, 1):
                for v in (-1, 1):
                    i = place(half, u, v, flip)
                    if u == 2:
                        got(i, p, 2 * half, 1)
                        got(i, p, 2 * half + 1, 1)
                    else:
                        got(i, p, 2 * half, 2)
                    push(i, p, 2 * half + (0 if v == -1 else 1), 1, nb(half, 1, -v))

    def e4(p):
        flip = p > 0
        for u in (0, -1, 1, 2):
            for half in (0, 1):
                i = place(half, u, 2, flip)
                got(i, p, 2 * half, 1)
                got(i, p, 2 * half + 1, 1)

    def swap(p):
        for half in (0, 1):
            push(me, p, 2 * half, 2, dev(0, 0, 1))

    def swapped(p):
        for half in (0, 1):
            got(dev(0, 0, 1), p, 2 * half, 2)

    owns = {}

    def ship(sig, slot, r, rows):
        n = chip(r)
        for k in (0, 1):
            to = 2 * n + (core if k == 0 else 1 - core)
            src, dst = send.at[sig, to, rows], recv.at[sig, ctx, rows]
            if r == 0 and k == 0:
                owns[slot] = pltpu.make_async_copy(src, dst, xr.at[slot, 0])
                owns[slot].start()
            else:
                remote(src, dst, xs.at[slot, 2 * r + k], xr.at[slot, 2 * r + k], (me, to))

    def exchanged(sig, slot, rows):
        owns[slot].wait()
        for r in range(4):
            for k in (0, 1):
                if r or k:
                    frm = 2 * chip(-r) + (core if k == 0 else 1 - core)
                    arrived(recv.at[sig, frm, rows], xr.at[slot, 2 * r + k])

    def dot(a, b):
        return jnp.dot(a, b, preferred_element_type=F32)

    def chunk(n):
        return pl.ds(pl.multiple_of(n * 256, 256), 256)

    def deliver(sig, slot, rows, make, at_once):
        for r in (2, 1, 3, 0):
            n = chip(r)
            z = make(chunk(n))
            send[sig, 2 * n, rows] = z[:, :128]
            send[sig, 2 * n + 1, rows] = z[:, 128:]
            go = functools.partial(ship, sig, slot, r, rows)
            if at_once:
                go()
            else:
                todo.append(go)

    def spread(sig, slot, rows, at_once=False):
        deliver(sig, slot, rows, lambda lanes: dot(cat[rows, :], perm[:, lanes]).astype(BF), at_once)

    def gathered(sig, rows):
        for d in range(CTX):
            cat[rows, d * 128:(d + 1) * 128] = recv[sig, d, rows]

    def collect(sig, use):
        gathered(sig, ALL)

        def body(n, _):
            z = dot(cat[...], perm[:, chunk(n)])
            use(2 * n, z[:, :128])
            use(2 * n + 1, z[:, 128:])
            return 0
        lax.fori_loop(0, 4, body, 0)

    def first_stage(sig, b0, nb):
        rows = pl.ds(b0, nb)
        gathered(sig, rows)

        def body(n, _):
            lanes = chunk(n)
            x = cat[rows, :]
            re = dot(x, kf[:, lanes])
            im = dot(x, kf[:, pl.ds(pl.multiple_of(1024 + n * 256, 256), 256)])
            c, s = twc[rows, lanes], tws[rows, lanes]
            turned[rows, lanes] = (re * c + im * s).astype(BF)
            turned[pl.ds(256 + b0, nb), lanes] = (im * c - re * s).astype(BF)
            return 0
        lax.fori_loop(0, 4, body, 0)

    def second_stage(sig):
        def body(n, _):
            lanes = chunk(n)
            spec[sig, :, lanes] = dot(tf[...], turned[:, lanes]).astype(BF)
            return 0
        lax.fori_loop(0, 4, body, 0)

    def inverse(first, second, conj, sig, at_once):
        def body(n, _):
            lanes = chunk(n)
            ar = spec[first, 0:256, lanes].astype(F32)
            ai = spec[first, 256:512, lanes].astype(F32)
            br = spec[second, 0:256, lanes].astype(F32)
            bi = spec[second, 256:512, lanes].astype(F32)
            if conj:
                pr, pi = ar * br + ai * bi, ar * bi - ai * br
            else:
                pr, pi = ar * br - ai * bi, ar * bi + ai * br
            p = jnp.concatenate([pr.astype(BF), pi.astype(BF)], 0)
            v = dot(ti[...], p)
            vr, vi = v[:256], v[256:]
            c, s = twc[:, lanes], tws[:, lanes]
            wide[:, lanes] = (vr * c - vi * s).astype(BF)
            wide[:, pl.ds(pl.multiple_of(1024 + n * 256, 256), 256)] = (vi * c + vr * s).astype(BF)
            return 0
        lax.fori_loop(0, 4, body, 0)
        deliver(
            sig, sig, ALL,
            lambda lanes: (dot(wide[...], ki[:, lanes]) * (1.0 / LEN)).astype(BF), at_once,
        )

    def upstream(p, lo=0, hi=8):
        flip = p > 0
        h = (1 - hh) if flip else hh
        b0, nb = PASSES[p]
        na = 256 // nb if nb < 256 else 1
        rows = pl.ds(b0, nb)

        def body(t, _):
            at = pl.ds(t * na, na)
            acc = up[at, rows, :].reshape(na * nb, 128) if flip else jnp.zeros((na * nb, 128), F32)
            for y in range(4):
                g = y * 2 + h
                x = jnp.concatenate(
                    [G[4 * g + k, at, rows, :].reshape(na * nb, 128) for k in range(4)], 1
                )
                acc = acc + dot(x, wt[g])
            up[at, rows, :] = acc.reshape(na, nb, 128)
            return 0
        lax.fori_loop(lo // na, hi // na, body, 0)

    def gate(p, slot, at_once):
        b0, nb = PASSES[p]
        rows = pl.ds(b0, nb)
        for a in range(8):
            cat[rows, a * 128:(a + 1) * 128] = (up[a, rows] * qkv[0, a, rows].astype(F32)).astype(BF)
        spread(2, slot, rows, at_once)

    def move(src, dst, k, to):
        pltpu.make_async_remote_copy(
            src_ref=src, dst_ref=dst, send_sem=rs.at[k], recv_sem=rr.at[k],
            device_id=(me, to), device_id_type=MESH,
        ).start()

    def half_part(r, b):
        g = jnp.concatenate(
            [G[4 * r + k, :, b:b + 128, :].reshape(1024, 128) for k in range(4)], 1
        )
        o = jnp.concatenate([out_t[:, a * 256 + b:a * 256 + b + 128] for a in range(8)], 1)
        return dot(o, g)

    def part_first():
        def body(y, _):
            psf[y] = half_part(2 * y + 1 - hh, 0)
            return 0
        lax.fori_loop(0, 4, body, 0)

    def part(flip):
        h = (1 - hh) if flip else hh

        def body(y, _):
            r = 2 * y + h
            if flip:
                z = psf[y] + half_part(r, 128)
            else:
                g = jnp.concatenate([G[4 * r + k].reshape(2048, 128) for k in range(4)], 1)
                z = dot(out_t[...], g)
            ps[r] = (z * (1.0 / math.sqrt(LEN))).astype(BF)
            return 0
        lax.fori_loop(0, 4, body, 0)

        @pl.when(core != h)
        def _():
            for r in (2, 1, 3, 0):
                move(ps.at[2 * chip(r) + h], pr1.at[r], r, sib)

    def combine(flip):
        h = (1 - hh) if flip else hh

        @pl.when(core == h)
        def _():
            for r in (2, 1, 3):
                arrived(pr1.at[r], rr.at[r])
                n = 2 * chip(r) + h
                ps2[r] = (ps[n].astype(F32) + pr1[r].astype(F32)).astype(BF)
                move(ps2.at[r], pr2.at[r], 3 + r, n)

    def weights_go(s):
        if s == 0:
            remote(W.at[ctx], W.at[ctx], ws.at[4], wr.at[4], (me, sib))
            for r in (2, 1, 3):
                todo.append(functools.partial(
                    remote, W.at[ctx], W.at[ctx], ws.at[r], wr.at[r], (me, 2 * chip(r) + core)
                ))
        if s == 2:
            for r in range(1, 4):
                frm = 2 * chip(-r) + core
                arrived(W.at[frm], wr.at[r])
                remote(W.at[frm], W.at[frm], ws.at[4 + r], wr.at[4 + r], (me, sib))

    def weights_in():
        arrived(W.at[sib], wr.at[4])
        for r in range(1, 4):
            arrived(W.at[2 * chip(-r) + 1 - core], wr.at[4 + r])

        def body(g, _):
            wt[g] = W[g].T
            return 0
        lax.fori_loop(0, CTX, body, 0)

    def use_conv(a, z):
        conv[a] = z.astype(BF)

    def turn(a, _):
        o = (qkv[0, a].astype(F32) * conv[a].astype(F32)).astype(BF)
        out_t[:, chunk(a)] = o.T
        return 0

    _, rows0, rows1 = (pl.ds(*q) for q in PASSES)

    loads["g"].wait()
    e0(0)
    swap(1)
    loads["qkv"].wait()
    loads["perm"].wait()
    for a in range(8):
        cat[:, a * 128:(a + 1) * 128] = (qkv[1, a].astype(F32) * qkv[2, a].astype(F32)).astype(BF)
    spread(0, 0, ALL)
    loads["tap"].wait()
    for a in range(8):
        cat[:, a * 128:(a + 1) * 128] = tap[a]
    spread(1, 1, ALL)
    todo.append(functools.partial(swap, 2))
    loads["w"].wait()
    weights_go(0)
    e1(0)
    e2(0)
    e3(0, (0,))
    for k in ("kf", "tf", "twc", "tws", "ki", "ti"):
        loads[k].wait()
    e3(0, (-1, 1))
    e3(0, (2,))
    flush()
    swapped(1)
    e0(1)
    swapped(2)
    e0(2)
    e4(0)
    exchanged(0, 0, ALL)
    first_stage(0, 0, 256)
    second_stage(0)
    e1(1)
    exchanged(1, 1, ALL)
    first_stage(1, 0, 256)
    second_stage(1)
    e2(1)
    inverse(1, 0, False, 3, False)
    e3(1, (0,))
    weights_go(2)
    e1(2)
    e3(1, (-1, 1))
    weights_in()
    upstream(0, 0, 4)
    e3(1, (2,))
    upstream(0, 4, 8)
    flush()
    e2(2)
    exchanged(3, 3, ALL)
    collect(3, use_conv)
    lax.fori_loop(0, 8, turn, 0)
    part(0)
    combine(0)
    e4(1)
    upstream(1)
    gate(1, 2, False)
    e3(2)
    flush()
    part_first()
    e4(2)
    upstream(2)
    gate(2, 6, True)
    part(1)
    combine(1)
    exchanged(2, 2, rows0)
    first_stage(2, *PASSES[1])

    exchanged(2, 6, rows1)
    first_stage(2, *PASSES[2])
    second_stage(2)
    early = list(sent)
    inverse(0, 2, True, 4, True)
    inverse(1, 2, True, 5, True)

    for a in range(8):
        outs[0, a] = (up[a] * conv[a].astype(F32)).astype(BF)
    writes = [pltpu.make_async_copy(outs.at[0], o_streams.at[0], osem.at[0])]
    writes[-1].start()

    arrived(pr1.at[0], rr.at[0])
    total = ps[ctx].astype(F32) + pr1[0].astype(F32)
    for r in range(1, 4):
        arrived(pr2.at[r], rr.at[3 + r])
        total = total + pr2[r].astype(F32)
    outw[...] = total
    writes.append(pltpu.make_async_copy(outw, o_weight, osem.at[1]))
    writes[-1].start()

    for copy in early:
        copy.wait_send()
    exchanged(4, 4, ALL)

    def use_taps(a, z):
        outs[1, a] = z.astype(BF)
    collect(4, use_taps)
    writes.append(pltpu.make_async_copy(outs.at[1], o_streams.at[1], osem.at[2]))
    writes[-1].start()

    exchanged(5, 5, ALL)

    def use_mix(a, z):
        outs[2, a] = z.astype(BF)
    collect(5, use_mix)
    writes.append(pltpu.make_async_copy(outs.at[2], o_streams.at[2], osem.at[3]))
    writes[-1].start()

    for copy in sent[len(early):]:
        copy.wait_send()
    for k in range(7):
        pltpu.make_async_remote_copy(
            src_ref=ps.at[0], dst_ref=pr1.at[0], send_sem=rs.at[k], recv_sem=rr.at[k],
            device_id=(me, sib), device_id_type=MESH,
        ).wait_send()
    for copy in writes:
        copy.wait()


def finish(found, key, value, weights, o_streams, o_filter, o_weight):
    o_streams[0] = found[0]
    o_filter[...] = found[1].astype(F32) * (1.0 / math.sqrt(LEN))
    mix = found[2].astype(F32)
    o_streams[1] = (mix * value[0].astype(F32)).astype(BF)
    o_streams[2] = (mix * key[0].astype(F32)).astype(BF)
    o_weight[...] = weights[...]


def shards(projected, filter_taps, out_grad, out_weight):
    consts = [jnp.asarray(t) for t in tables()]
    vm = pltpu.VMEM
    sem = pltpu.SemaphoreType.DMA
    found, weights = pl.pallas_call(
        kernel,
        out_shape=(
            jax.ShapeDtypeStruct((3, 8, 256, 128), BF),
            jax.ShapeDtypeStruct((128, 512), F32),
        ),
        in_specs=[pl.BlockSpec(memory_space=pl.ANY)] * 11,
        out_specs=(pl.BlockSpec(memory_space=pl.ANY),) * 2,
        scratch_shapes=[
            vm((3, 8, 256, 128), BF),
            vm((8, 256, 128), BF),
            vm((32, 8, 256, 128), BF),
            vm((8, 128, 512), BF),
            vm((8, 512, 128), BF),
            vm((1024, 1024), BF),
            vm((1024, 2048), BF),
            vm((2048, 1024), BF),
            vm((512, 512), BF),
            vm((512, 512), BF),
            vm((256, 1024), F32),
            vm((256, 1024), F32),
            vm((256, 1024), BF),
            vm((6, 8, 256, 128), BF),
            vm((6, 8, 256, 128), BF),
            vm((3, 512, 1024), BF),
            vm((512, 1024), BF),
            vm((256, 2048), BF),
            vm((8, 256, 128), F32),
            vm((8, 256, 128), BF),
            vm((128, 2048), BF),
            vm((8, 128, 512), BF),
            vm((4, 128, 512), F32),
            vm((4, 128, 512), BF),
            vm((4, 128, 512), BF),
            vm((4, 128, 512), BF),
            vm((3, 8, 256, 128), BF),
            vm((128, 512), F32),
            sem((11,)), sem((5,)),
            sem((184,)), sem((32, 8)),
            sem((7, 8)), sem((7, 8)),
            sem((13,)), sem((8,)),
            sem((8,)), sem((8,)),
        ],
        compiler_params=pltpu.CompilerParams(
            collective_id=0, has_side_effects=True, vmem_limit_bytes=60 * 2**20
        ),
    )(
        projected.reshape(3, 8, 256, 128), filter_taps.reshape(8, 256, 128),
        out_grad.reshape(8, 256, 128), out_weight, *consts,
    )
    rows = pl.BlockSpec((3, 1024, 128), lambda i: (0, i, 0))
    keys = pl.BlockSpec((1, 1024, 128), lambda i: (1, i, 0))
    values = pl.BlockSpec((1, 1024, 128), lambda i: (2, i, 0))
    part = pl.BlockSpec((64, 512), lambda i: (i, 0))
    return pl.pallas_call(
        finish,
        grid=(2,),
        out_shape=(
            jax.ShapeDtypeStruct((3, 2048, 128), BF),
            jax.ShapeDtypeStruct((2048, 128), F32),
            jax.ShapeDtypeStruct((128, 512), F32),
        ),
        in_specs=[rows, keys, values, part],
        out_specs=(rows, pl.BlockSpec((1024, 128), lambda i: (i, 0)), part),
    )(found.reshape(3, 2048, 128), projected, projected, weights)


def solution(mesh):
    placed = (P(None, "context", "dp"), P("context", "dp"), P("context", "dp"), P("dp", "context"))
    return jax.shard_map(
        shards,
        mesh=mesh,
        in_specs=placed,
        out_specs=(P(None, "context", "dp"), P("context", "dp"), P("dp", "context")),
        check_vma=False,
    )
```

```python
import functools
import math

import jax
import jax.numpy as jnp
import ml_dtypes
import numpy as np
from jax import lax
from jax.experimental import pallas as pl
from jax.experimental.pallas import tpu as pltpu
from jax.sharding import PartitionSpec as P

CTX = 8
ROWS = 256
STEPS = 64
CH = 16
LEN = 16384
F32 = jnp.float32
BF = jnp.bfloat16
MESH = pl.DeviceIdType.MESH
ALL = pl.ds(0, ROWS)
PASSES = ((0, 256), (0, 128), (128, 64), (192, 64))
PACE = 3


def tables():
    s = np.arange(STEPS)
    klo = np.arange(STEPS) + 0.25
    th = 2 * np.pi * s[:, None] * klo[None, :] / STEPS
    eye = np.eye(CH)
    fwd = np.concatenate([np.kron(np.cos(th), eye), np.kron(-np.sin(th), eye)], 1)
    b = np.arange(ROWS)
    ph = 2 * np.pi * ((b[:, None] * b[None, :]) % ROWS) / ROWS
    c, sn = np.cos(ph), np.sin(ph)
    tf = np.block([[c, sn], [-sn, c]])
    ps = 2 * np.pi * b[:, None] * klo[None, :] / LEN
    twc = np.repeat(np.cos(ps), CH, axis=1).astype(np.float32)
    tws = np.repeat(np.sin(ps), CH, axis=1).astype(np.float32)
    perm = np.zeros((8, 8, CH, 8, 8, CH), np.float32)
    for a in range(8):
        for g in range(8):
            for k in range(CH):
                perm[a, g, k, g, a, k] = 1
    perm = perm.reshape(1024, 1024)
    low = lambda z: np.ascontiguousarray(z).astype(ml_dtypes.bfloat16)
    return low(perm), low(fwd), low(fwd.T), low(tf), low(tf.T), twc, tws


def kernel(
    proj, taps, grad, weight, perm_h, kf_h, ki_h, tf_h, ti_h, twc_h, tws_h,
    o_streams, o_weight,
    qkv, tap, G, W, wt, perm, kf, ki, tf, ti, twc, tws,
    cat, send, recv, spec, turned, wide, up, conv, out_t,
    ps, psf, ps2, pr1, pr2, outs, outw,
    lsem, osem, gs, gr, xs, xr, ws, wr, rs, rr,
):
    me = lax.axis_index("dp")
    ctx = lax.axis_index("context")
    yy, hh, xx = me // 8, (me // 4) % 2, me % 4
    zz, core = ctx // 2, ctx % 2
    sib = ctx + 1 - 2 * core

    def dev(dy, dx, flip):
        h = (1 - hh) if flip else hh
        return (lax.rem(yy + dy + 4, 4) * 2 + h) * 4 + lax.rem(xx + dx + 4, 4)

    def chip(r):
        return lax.rem(zz + r + 4, 4)

    loads = {}

    def load(name, src, dst, k):
        loads[name] = pltpu.make_async_copy(src, dst, lsem.at[k])
        loads[name].start()

    load("g", grad, G.at[me], 0)
    load("qkv", proj, qkv, 2)
    load("perm", perm_h, perm, 3)
    load("tap", taps, tap, 4)
    load("w", weight, W.at[ctx], 1)
    load("kf", kf_h, kf, 5)
    load("tf", tf_h, tf, 6)
    load("twc", twc_h, twc, 7)
    load("tws", tws_h, tws, 8)
    load("ki", ki_h, ki, 9)
    load("ti", ti_h, ti, 10)

    bar = pltpu.get_barrier_semaphore()
    for r in range(1, CTX):
        pl.semaphore_signal(bar, inc=1, device_id=(me, lax.rem(ctx + r, CTX)), device_id_type=MESH)
    for d in (dev(0, 1, 0), dev(0, -1, 0), dev(1, 0, 0), dev(-1, 0, 0), dev(0, 0, 1)):
        pl.semaphore_signal(bar, inc=1, device_id=(d, ctx), device_id_type=MESH)
    pl.semaphore_wait(bar, CTX - 1 + 5)

    sent = []

    def remote(src, dst, ssem, rsem, where):
        copy = pltpu.make_async_remote_copy(
            src_ref=src, dst_ref=dst, send_sem=ssem, recv_sem=rsem,
            device_id=where, device_id_type=MESH,
        )
        copy.start()
        sent.append(copy)

    def arrived(buf, rsem):
        pltpu.make_async_remote_copy(
            src_ref=buf, dst_ref=buf, send_sem=gs.at[0], recv_sem=rsem,
            device_id=(me, sib), device_id_type=MESH,
        ).wait_recv()

    nsend = [0]
    todo = []

    def flush():
        while todo:
            todo.pop(0)()

    def piece(i, p, q, n):
        b0, nb = PASSES[p]
        return G.at[i, :, pl.ds(b0 + q * (nb // 4), n * (nb // 4)), :]

    def push(i, p, q, n, to):
        k = nsend[0]
        nsend[0] += 1
        r = piece(i, p, q, n)
        remote(r, r, gs.at[k], gr.at[i, 4 * max(p - 1, 0) + q], (to, ctx))
        if todo and k % PACE == PACE - 1:
            todo.pop(0)()

    def got(i, p, q, n):
        arrived(piece(i, p, q, n), gr.at[i, 4 * max(p - 1, 0) + q])

    def place(half, u, v, flip):
        return dev(v, u, flip) if half == 0 else dev(u, v, flip)

    def nb(half, axis, step):
        return place(half, step, 0, 0) if axis == 0 else place(half, 0, step, 0)

    def e0(p):
        flip = p > 0
        src = dev(0, 0, flip)
        for axis in (0, 1):
            for half in (0, 1):
                for step in (1, -1):
                    push(src, p, 2 * half, 2, nb(half, axis, step))

    def e1(p):
        flip = p > 0
        for half in (0, 1):
            for u in (-1, 1):
                i = place(half, u, 0, flip)
                got(i, p, 2 * half, 2)
                push(i, p, 2 * half + (0 if u == -1 else 1), 1, nb(half, 0, -u))
        for u in (-1, 1):
            for half in (0, 1):
                for step in (1, -1):
                    push(place(half, u, 0, flip), p, 2 * half, 2, nb(half, 1, step))

    def e2(p):
        flip = p > 0
        for q in (0, 1):
            for half in (0, 1):
                i = place(half, 2, 0, flip)
                got(i, p, 2 * half + q, 1)
                for step in (1, -1):
                    push(i, p, 2 * half + q, 1, nb(half, 1, step))

    def e3(p, us=(0, -1, 1, 2)):
        flip = p > 0
        for u in us:
            for half in (0, 1):
                for v in (-1, 1):
                    i = place(half, u, v, flip)
                    if u == 2:
                        got(i, p, 2 * half, 1)
                        got(i, p, 2 * half + 1, 1)
                    else:
                        got(i, p, 2 * half, 2)
                    push(i, p, 2 * half + (0 if v == -1 else 1), 1, nb(half, 1, -v))

    def e4(p):
        flip = p > 0
        for u in (0, -1, 1, 2):
            for half in (0, 1):
                i = place(half, u, 2, flip)
                got(i, p, 2 * half, 1)
                got(i, p, 2 * half + 1, 1)

    def swap(p):
        for half in (0, 1):
            push(me, p, 2 * half, 2, dev(0, 0, 1))

    def swapped(p):
        for half in (0, 1):
            got(dev(0, 0, 1), p, 2 * half, 2)

    owns = {}

    def ship(sig, slot, r, rows):
        n = chip(r)
        for k in (0, 1):
            to = 2 * n + (core if k == 0 else 1 - core)
            src, dst = send.at[sig, to, rows], recv.at[sig, ctx, rows]
            if r == 0 and k == 0:
                owns[slot] = pltpu.make_async_copy(src, dst, xr.at[slot, 0])
                owns[slot].start()
            else:
                remote(src, dst, xs.at[slot, 2 * r + k], xr.at[slot, 2 * r + k], (me, to))

    def exchanged(sig, slot, rows):
        owns[slot].wait()
        for r in range(4):
            for k in (0, 1):
                if r or k:
                    frm = 2 * chip(-r) + (core if k == 0 else 1 - core)
                    arrived(recv.at[sig, frm, rows], xr.at[slot, 2 * r + k])

    def dot(a, b):
        return jnp.dot(a, b, preferred_element_type=F32)

    def chunk(n):
        return pl.ds(pl.multiple_of(n * 256, 256), 256)

    def deliver(sig, slot, rows, make, at_once):
        for r in (2, 1, 3, 0):
            n = chip(r)
            z = make(chunk(n))
            send[sig, 2 * n, rows] = z[:, :128]
            send[sig, 2 * n + 1, rows] = z[:, 128:]
            go = functools.partial(ship, sig, slot, r, rows)
            if at_once:
                go()
            else:
                todo.append(go)

    def spread(sig, slot, rows, at_once=False):
        deliver(sig, slot, rows, lambda lanes: dot(cat[rows, :], perm[:, lanes]).astype(BF), at_once)

    def gathered(sig, rows):
        for d in range(CTX):
            cat[rows, d * 128:(d + 1) * 128] = recv[sig, d, rows]

    def collect(sig, use):
        gathered(sig, ALL)

        def body(n, _):
            z = dot(cat[...], perm[:, chunk(n)])
            use(2 * n, z[:, :128])
            use(2 * n + 1, z[:, 128:])
            return 0
        lax.fori_loop(0, 4, body, 0)

    def first_stage(sig, b0, nb):
        rows = pl.ds(b0, nb)
        gathered(sig, rows)

        def body(n, _):
            lanes = chunk(n)
            x = cat[rows, :]
            re = dot(x, kf[:, lanes])
            im = dot(x, kf[:, pl.ds(pl.multiple_of(1024 + n * 256, 256), 256)])
            c, s = twc[rows, lanes], tws[rows, lanes]
            turned[rows, lanes] = (re * c + im * s).astype(BF)
            turned[pl.ds(256 + b0, nb), lanes] = (im * c - re * s).astype(BF)
            return 0
        lax.fori_loop(0, 4, body, 0)

    def second_stage(sig):
        def body(n, _):
            lanes = chunk(n)
            spec[sig, :, lanes] = dot(tf[...], turned[:, lanes]).astype(BF)
            return 0
        lax.fori_loop(0, 4, body, 0)

    def inverse(first, second, conj, sig, at_once):
        def body(n, _):
            lanes = chunk(n)
            ar = spec[first, 0:256, lanes].astype(F32)
            ai = spec[first, 256:512, lanes].astype(F32)
            br = spec[second, 0:256, lanes].astype(F32)
            bi = spec[second, 256:512, lanes].astype(F32)
            if conj:
                pr, pi = ar * br + ai * bi, ar * bi - ai * br
            else:
                pr, pi = ar * br - ai * bi, ar * bi + ai * br
            p = jnp.concatenate([pr.astype(BF), pi.astype(BF)], 0)
            v = dot(ti[...], p)
            vr, vi = v[:256], v[256:]
            c, s = twc[:, lanes], tws[:, lanes]
            wide[:, lanes] = (vr * c - vi * s).astype(BF)
            wide[:, pl.ds(pl.multiple_of(1024 + n * 256, 256), 256)] = (vi * c + vr * s).astype(BF)
            return 0
        lax.fori_loop(0, 4, body, 0)
        deliver(
            sig, sig, ALL,
            lambda lanes: (dot(wide[...], ki[:, lanes]) * (1.0 / LEN)).astype(BF), at_once,
        )

    def upstream(p, lo=0, hi=8):
        flip = p > 0
        h = (1 - hh) if flip else hh
        b0, nb = PASSES[p]
        na = 256 // nb if nb < 256 else 1
        rows = pl.ds(b0, nb)

        def body(t, _):
            at = pl.ds(t * na, na)
            acc = up[at, rows, :].reshape(na * nb, 128) if flip else jnp.zeros((na * nb, 128), F32)
            for y in range(4):
                g = y * 2 + h
                x = jnp.concatenate(
                    [G[4 * g + k, at, rows, :].reshape(na * nb, 128) for k in range(4)], 1
                )
                acc = acc + dot(x, wt[g])
            up[at, rows, :] = acc.reshape(na, nb, 128)
            return 0
        lax.fori_loop(lo // na, hi // na, body, 0)

    def gate(p, slot, at_once):
        b0, nb = PASSES[p]
        rows = pl.ds(b0, nb)
        for a in range(8):
            cat[rows, a * 128:(a + 1) * 128] = (up[a, rows] * qkv[0, a, rows].astype(F32)).astype(BF)
        spread(2, slot, rows, at_once)

    def move(src, dst, k, to):
        pltpu.make_async_remote_copy(
            src_ref=src, dst_ref=dst, send_sem=rs.at[k], recv_sem=rr.at[k],
            device_id=(me, to), device_id_type=MESH,
        ).start()

    def half_part(r, b):
        g = jnp.concatenate(
            [G[4 * r + k, :, b:b + 128, :].reshape(1024, 128) for k in range(4)], 1
        )
        o = jnp.concatenate([out_t[:, a * 256 + b:a * 256 + b + 128] for a in range(8)], 1)
        return dot(o, g)

    def part_first():
        def body(y, _):
            psf[y] = half_part(2 * y + 1 - hh, 0)
            return 0
        lax.fori_loop(0, 4, body, 0)

    def part(flip):
        h = (1 - hh) if flip else hh

        def body(y, _):
            r = 2 * y + h
            if flip:
                z = psf[y] + half_part(r, 128)
            else:
                g = jnp.concatenate([G[4 * r + k].reshape(2048, 128) for k in range(4)], 1)
                z = dot(out_t[...], g)
            ps[r] = (z * (1.0 / math.sqrt(LEN))).astype(BF)
            return 0
        lax.fori_loop(0, 4, body, 0)

        @pl.when(core != h)
        def _():
            for r in (2, 1, 3, 0):
                move(ps.at[2 * chip(r) + h], pr1.at[r], r, sib)

    def combine(flip):
        h = (1 - hh) if flip else hh

        @pl.when(core == h)
        def _():
            for r in (2, 1, 3):
                arrived(pr1.at[r], rr.at[r])
                n = 2 * chip(r) + h
                ps2[r] = (ps[n].astype(F32) + pr1[r].astype(F32)).astype(BF)
                move(ps2.at[r], pr2.at[r], 3 + r, n)

    def weights_go(s):
        if s == 0:
            remote(W.at[ctx], W.at[ctx], ws.at[4], wr.at[4], (me, sib))
            for r in (2, 1, 3):
                todo.append(functools.partial(
                    remote, W.at[ctx], W.at[ctx], ws.at[r], wr.at[r], (me, 2 * chip(r) + core)
                ))
        if s == 2:
            for r in range(1, 4):
                frm = 2 * chip(-r) + core
                arrived(W.at[frm], wr.at[r])
                remote(W.at[frm], W.at[frm], ws.at[4 + r], wr.at[4 + r], (me, sib))

    def weights_in():
        arrived(W.at[sib], wr.at[4])
        for r in range(1, 4):
            arrived(W.at[2 * chip(-r) + 1 - core], wr.at[4 + r])

        def body(g, _):
            wt[g] = W[g].T
            return 0
        lax.fori_loop(0, CTX, body, 0)

    def use_conv(a, z):
        conv[a] = z.astype(BF)

    def turn(a, _):
        o = (qkv[0, a].astype(F32) * conv[a].astype(F32)).astype(BF)
        out_t[:, chunk(a)] = o.T
        return 0

    _, rows0, rows1, rows2 = (pl.ds(*q) for q in PASSES)

    loads["g"].wait()
    e0(0)
    swap(1)
    swap(2)
    swap(3)
    loads["qkv"].wait()
    loads["perm"].wait()
    for a in range(8):
        cat[:, a * 128:(a + 1) * 128] = (qkv[1, a].astype(F32) * qkv[2, a].astype(F32)).astype(BF)
    spread(0, 0, ALL)
    loads["tap"].wait()
    for a in range(8):
        cat[:, a * 128:(a + 1) * 128] = tap[a]
    spread(1, 1, ALL)
    loads["w"].wait()
    weights_go(0)
    e1(0)
    e2(0)
    e3(0, (0,))
    for k in ("kf", "tf", "twc", "tws", "ki", "ti"):
        loads[k].wait()
    e3(0, (-1, 1))
    e3(0, (2,))
    flush()
    swapped(1)
    e0(1)
    e4(0)
    exchanged(0, 0, ALL)
    first_stage(0, 0, 256)
    second_stage(0)
    e1(1)
    swapped(2)
    e0(2)
    exchanged(1, 1, ALL)
    first_stage(1, 0, 256)
    second_stage(1)
    e2(1)
    inverse(1, 0, False, 3, False)
    e3(1, (0,))
    weights_go(2)
    swapped(3)
    e0(3)
    e1(2)
    e3(1, (-1, 1))
    weights_in()
    upstream(0, 0, 4)
    e3(1, (2,))
    upstream(0, 4, 8)
    flush()
    e2(2)
    e1(3)
    exchanged(3, 3, ALL)
    collect(3, use_conv)
    lax.fori_loop(0, 8, turn, 0)
    part(0)
    combine(0)
    e4(1)
    upstream(1)
    gate(1, 2, False)
    e3(2)
    e2(3)
    flush()
    e4(2)
    upstream(2)
    gate(2, 6, False)
    e3(3)
    flush()
    part_first()
    exchanged(2, 2, rows0)
    first_stage(2, *PASSES[1])
    e4(3)
    upstream(3)
    gate(3, 7, True)
    part(1)
    combine(1)
    exchanged(2, 6, rows1)
    first_stage(2, *PASSES[2])

    exchanged(2, 7, rows2)
    first_stage(2, *PASSES[3])
    second_stage(2)
    early = list(sent)
    inverse(0, 2, True, 4, True)
    inverse(1, 2, True, 5, True)

    for a in range(8):
        outs[0, a] = (up[a] * conv[a].astype(F32)).astype(BF)
    writes = [pltpu.make_async_copy(outs.at[0], o_streams.at[0], osem.at[0])]
    writes[-1].start()

    arrived(pr1.at[0], rr.at[0])
    total = ps[ctx].astype(F32) + pr1[0].astype(F32)
    for r in range(1, 4):
        arrived(pr2.at[r], rr.at[3 + r])
        total = total + pr2[r].astype(F32)
    outw[...] = total
    writes.append(pltpu.make_async_copy(outw, o_weight, osem.at[1]))
    writes[-1].start()

    for copy in early:
        copy.wait_send()
    exchanged(4, 4, ALL)

    def use_taps(a, z):
        outs[1, a] = z.astype(BF)
    collect(4, use_taps)
    writes.append(pltpu.make_async_copy(outs.at[1], o_streams.at[1], osem.at[2]))
    writes[-1].start()

    exchanged(5, 5, ALL)

    def use_mix(a, z):
        outs[2, a] = z.astype(BF)
    collect(5, use_mix)
    writes.append(pltpu.make_async_copy(outs.at[2], o_streams.at[2], osem.at[3]))
    writes[-1].start()

    for copy in sent[len(early):]:
        copy.wait_send()
    for k in range(7):
        pltpu.make_async_remote_copy(
            src_ref=ps.at[0], dst_ref=pr1.at[0], send_sem=rs.at[k], recv_sem=rr.at[k],
            device_id=(me, sib), device_id_type=MESH,
        ).wait_send()
    for copy in writes:
        copy.wait()


def finish(found, key, value, weights, o_streams, o_filter, o_weight):
    o_streams[0] = found[0]
    o_filter[...] = found[1].astype(F32) * (1.0 / math.sqrt(LEN))
    mix = found[2].astype(F32)
    o_streams[1] = (mix * value[0].astype(F32)).astype(BF)
    o_streams[2] = (mix * key[0].astype(F32)).astype(BF)
    o_weight[...] = weights[...]


def shards(projected, filter_taps, out_grad, out_weight):
    consts = [jnp.asarray(t) for t in tables()]
    vm = pltpu.VMEM
    sem = pltpu.SemaphoreType.DMA
    found, weights = pl.pallas_call(
        kernel,
        out_shape=(
            jax.ShapeDtypeStruct((3, 8, 256, 128), BF),
            jax.ShapeDtypeStruct((128, 512), F32),
        ),
        in_specs=[pl.BlockSpec(memory_space=pl.ANY)] * 11,
        out_specs=(pl.BlockSpec(memory_space=pl.ANY),) * 2,
        scratch_shapes=[
            vm((3, 8, 256, 128), BF),
            vm((8, 256, 128), BF),
            vm((32, 8, 256, 128), BF),
            vm((8, 128, 512), BF),
            vm((8, 512, 128), BF),
            vm((1024, 1024), BF),
            vm((1024, 2048), BF),
            vm((2048, 1024), BF),
            vm((512, 512), BF),
            vm((512, 512), BF),
            vm((256, 1024), F32),
            vm((256, 1024), F32),
            vm((256, 1024), BF),
            vm((6, 8, 256, 128), BF),
            vm((6, 8, 256, 128), BF),
            vm((3, 512, 1024), BF),
            vm((512, 1024), BF),
            vm((256, 2048), BF),
            vm((8, 256, 128), F32),
            vm((8, 256, 128), BF),
            vm((128, 2048), BF),
            vm((8, 128, 512), BF),
            vm((4, 128, 512), F32),
            vm((4, 128, 512), BF),
            vm((4, 128, 512), BF),
            vm((4, 128, 512), BF),
            vm((3, 8, 256, 128), BF),
            vm((128, 512), F32),
            sem((11,)), sem((5,)),
            sem((184,)), sem((32, 12)),
            sem((8, 8)), sem((8, 8)),
            sem((13,)), sem((8,)),
            sem((8,)), sem((8,)),
        ],
        compiler_params=pltpu.CompilerParams(
            collective_id=0, has_side_effects=True, vmem_limit_bytes=60 * 2**20
        ),
    )(
        projected.reshape(3, 8, 256, 128), filter_taps.reshape(8, 256, 128),
        out_grad.reshape(8, 256, 128), out_weight, *consts,
    )
    rows = pl.BlockSpec((3, 1024, 128), lambda i: (0, i, 0))
    keys = pl.BlockSpec((1, 1024, 128), lambda i: (1, i, 0))
    values = pl.BlockSpec((1, 1024, 128), lambda i: (2, i, 0))
    part = pl.BlockSpec((64, 512), lambda i: (i, 0))
    return pl.pallas_call(
        finish,
        grid=(2,),
        out_shape=(
            jax.ShapeDtypeStruct((3, 2048, 128), BF),
            jax.ShapeDtypeStruct((2048, 128), F32),
            jax.ShapeDtypeStruct((128, 512), F32),
        ),
        in_specs=[rows, keys, values, part],
        out_specs=(rows, pl.BlockSpec((1024, 128), lambda i: (i, 0)), part),
    )(found.reshape(3, 2048, 128), projected, projected, weights)


def solution(mesh):
    placed = (P(None, "context", "dp"), P("context", "dp"), P("context", "dp"), P("dp", "context"))
    return jax.shard_map(
        shards,
        mesh=mesh,
        in_specs=placed,
        out_specs=(P(None, "context", "dp"), P("context", "dp"), P("dp", "context")),
        check_vma=False,
    )
```

```python
import functools
import math

import jax
import jax.numpy as jnp
import ml_dtypes
import numpy as np
from jax import lax
from jax.experimental import pallas as pl
from jax.experimental.pallas import tpu as pltpu
from jax.sharding import PartitionSpec as P

CTX = 8
ROWS = 256
STEPS = 64
CH = 16
LEN = 16384
F32 = jnp.float32
BF = jnp.bfloat16
MESH = pl.DeviceIdType.MESH
ALL = pl.ds(0, ROWS)
PASSES = ((0, 256), (0, 128), (128, 64), (192, 64))
PACE = 3


def tables():
    s = np.arange(STEPS)
    klo = np.arange(STEPS) + 0.25
    th = 2 * np.pi * s[:, None] * klo[None, :] / STEPS
    eye = np.eye(CH)
    fwd = np.concatenate([np.kron(np.cos(th), eye), np.kron(-np.sin(th), eye)], 1)
    b = np.arange(ROWS)
    ph = 2 * np.pi * ((b[:, None] * b[None, :]) % ROWS) / ROWS
    c, sn = np.cos(ph), np.sin(ph)
    tf = np.block([[c, sn], [-sn, c]])
    ps = 2 * np.pi * b[:, None] * klo[None, :] / LEN
    twc = np.repeat(np.cos(ps), CH, axis=1).astype(np.float32)
    tws = np.repeat(np.sin(ps), CH, axis=1).astype(np.float32)
    perm = np.zeros((8, 8, CH, 8, 8, CH), np.float32)
    for a in range(8):
        for g in range(8):
            for k in range(CH):
                perm[a, g, k, g, a, k] = 1
    perm = perm.reshape(1024, 1024)
    low = lambda z: np.ascontiguousarray(z).astype(ml_dtypes.bfloat16)
    return low(perm), low(fwd), low(fwd.T), low(tf), low(tf.T), twc, tws


def kernel(
    proj, taps, grad, weight, perm_h, kf_h, ki_h, tf_h, ti_h, twc_h, tws_h,
    o_streams, o_weight,
    qkv, tap, G, W, wt, perm, kf, ki, tf, ti, twc, tws,
    cat, send, recv, spec, turned, wide, up, conv, out_t,
    ps, psf, ps2, pr1, pr2, outs, outw,
    lsem, osem, gs, gr, xs, xr, ws, wr, rs, rr,
):
    me = lax.axis_index("dp")
    ctx = lax.axis_index("context")
    yy, hh, xx = me // 8, (me // 4) % 2, me % 4
    zz, core = ctx // 2, ctx % 2
    sib = ctx + 1 - 2 * core

    def dev(dy, dx, flip):
        h = (1 - hh) if flip else hh
        return (lax.rem(yy + dy + 4, 4) * 2 + h) * 4 + lax.rem(xx + dx + 4, 4)

    def chip(r):
        return lax.rem(zz + r + 4, 4)

    loads = {}

    def load(name, src, dst, k):
        loads[name] = pltpu.make_async_copy(src, dst, lsem.at[k])
        loads[name].start()

    load("g", grad, G.at[me], 0)
    load("qkv", proj, qkv, 2)
    load("perm", perm_h, perm, 3)
    load("tap", taps, tap, 4)
    load("w", weight, W.at[ctx], 1)
    load("kf", kf_h, kf, 5)
    load("tf", tf_h, tf, 6)
    load("twc", twc_h, twc, 7)
    load("tws", tws_h, tws, 8)
    load("ki", ki_h, ki, 9)
    load("ti", ti_h, ti, 10)

    bar = pltpu.get_barrier_semaphore()
    for r in range(1, CTX):
        pl.semaphore_signal(bar, inc=1, device_id=(me, lax.rem(ctx + r, CTX)), device_id_type=MESH)
    for d in (dev(0, 1, 0), dev(0, -1, 0), dev(1, 0, 0), dev(-1, 0, 0), dev(0, 0, 1)):
        pl.semaphore_signal(bar, inc=1, device_id=(d, ctx), device_id_type=MESH)
    pl.semaphore_wait(bar, CTX - 1 + 5)

    sent = []

    def remote(src, dst, ssem, rsem, where):
        copy = pltpu.make_async_remote_copy(
            src_ref=src, dst_ref=dst, send_sem=ssem, recv_sem=rsem,
            device_id=where, device_id_type=MESH,
        )
        copy.start()
        sent.append(copy)

    def arrived(buf, rsem):
        pltpu.make_async_remote_copy(
            src_ref=buf, dst_ref=buf, send_sem=gs.at[0], recv_sem=rsem,
            device_id=(me, sib), device_id_type=MESH,
        ).wait_recv()

    nsend = [0]
    todo = []

    def flush():
        while todo:
            todo.pop(0)()

    def piece(i, p, q, n):
        b0, nb = PASSES[p]
        return G.at[i, :, pl.ds(b0 + q * (nb // 4), n * (nb // 4)), :]

    def push(i, p, q, n, to):
        k = nsend[0]
        nsend[0] += 1
        r = piece(i, p, q, n)
        remote(r, r, gs.at[k], gr.at[i, 4 * max(p - 1, 0) + q], (to, ctx))
        if todo and k % PACE == PACE - 1:
            todo.pop(0)()

    def got(i, p, q, n):
        arrived(piece(i, p, q, n), gr.at[i, 4 * max(p - 1, 0) + q])

    def place(half, u, v, flip):
        return dev(v, u, flip) if half == 0 else dev(u, v, flip)

    def nb(half, axis, step):
        return place(half, step, 0, 0) if axis == 0 else place(half, 0, step, 0)

    def e0(p):
        flip = p > 0
        src = dev(0, 0, flip)
        for axis in (0, 1):
            for half in (0, 1):
                for step in (1, -1):
                    push(src, p, 2 * half, 2, nb(half, axis, step))

    def e1(p):
        flip = p > 0
        for half in (0, 1):
            for u in (-1, 1):
                i = place(half, u, 0, flip)
                got(i, p, 2 * half, 2)
                push(i, p, 2 * half + (0 if u == -1 else 1), 1, nb(half, 0, -u))
        for u in (-1, 1):
            for half in (0, 1):
                for step in (1, -1):
                    push(place(half, u, 0, flip), p, 2 * half, 2, nb(half, 1, step))

    def e2(p):
        flip = p > 0
        for q in (0, 1):
            for half in (0, 1):
                i = place(half, 2, 0, flip)
                got(i, p, 2 * half + q, 1)
                for step in (1, -1):
                    push(i, p, 2 * half + q, 1, nb(half, 1, step))

    def e3(p, us=(0, -1, 1, 2)):
        flip = p > 0
        for u in us:
            for half in (0, 1):
                for v in (-1, 1):
                    i = place(half, u, v, flip)
                    if u == 2:
                        got(i, p, 2 * half, 1)
                        got(i, p, 2 * half + 1, 1)
                    else:
                        got(i, p, 2 * half, 2)
                    push(i, p, 2 * half + (0 if v == -1 else 1), 1, nb(half, 1, -v))

    def e4(p):
        flip = p > 0
        for u in (0, -1, 1, 2):
            for half in (0, 1):
                i = place(half, u, 2, flip)
                got(i, p, 2 * half, 1)
                got(i, p, 2 * half + 1, 1)

    def swap(p):
        for half in (0, 1):
            push(me, p, 2 * half, 2, dev(0, 0, 1))

    def swapped(p):
        for half in (0, 1):
            got(dev(0, 0, 1), p, 2 * half, 2)

    owns = {}

    def ship(sig, slot, r, rows):
        n = chip(r)
        for k in (0, 1):
            to = 2 * n + (core if k == 0 else 1 - core)
            src, dst = send.at[sig, to, rows], recv.at[sig, ctx, rows]
            if r == 0 and k == 0:
                owns[slot] = pltpu.make_async_copy(src, dst, xr.at[slot, 0])
                owns[slot].start()
            else:
                remote(src, dst, xs.at[slot, 2 * r + k], xr.at[slot, 2 * r + k], (me, to))

    def exchanged(sig, slot, rows):
        owns[slot].wait()
        for r in range(4):
            for k in (0, 1):
                if r or k:
                    frm = 2 * chip(-r) + (core if k == 0 else 1 - core)
                    arrived(recv.at[sig, frm, rows], xr.at[slot, 2 * r + k])

    def dot(a, b):
        return jnp.dot(a, b, preferred_element_type=F32)

    def chunk(n):
        return pl.ds(pl.multiple_of(n * 256, 256), 256)

    def deliver(sig, slot, rows, make, at_once):
        for r in (2, 1, 3, 0):
            n = chip(r)
            z = make(chunk(n))
            send[sig, 2 * n, rows] = z[:, :128]
            send[sig, 2 * n + 1, rows] = z[:, 128:]
            go = functools.partial(ship, sig, slot, r, rows)
            if at_once:
                go()
            else:
                todo.append(go)

    def spread(sig, slot, rows, at_once=False):
        deliver(sig, slot, rows, lambda lanes: dot(cat[rows, :], perm[:, lanes]).astype(BF), at_once)

    def gathered(sig, rows):
        for d in range(CTX):
            cat[rows, d * 128:(d + 1) * 128] = recv[sig, d, rows]

    def collect(sig, use):
        gathered(sig, ALL)

        def body(n, _):
            z = dot(cat[...], perm[:, chunk(n)])
            use(2 * n, z[:, :128])
            use(2 * n + 1, z[:, 128:])
            return 0
        lax.fori_loop(0, 4, body, 0)

    def first_stage(sig, b0, nb):
        rows = pl.ds(b0, nb)
        gathered(sig, rows)

        def body(n, _):
            lanes = chunk(n)
            x = cat[rows, :]
            re = dot(x, kf[:, lanes])
            im = dot(x, kf[:, pl.ds(pl.multiple_of(1024 + n * 256, 256), 256)])
            c, s = twc[rows, lanes], tws[rows, lanes]
            turned[rows, lanes] = (re * c + im * s).astype(BF)
            turned[pl.ds(256 + b0, nb), lanes] = (im * c - re * s).astype(BF)
            return 0
        lax.fori_loop(0, 4, body, 0)

    def second_stage(sig):
        def body(n, _):
            lanes = chunk(n)
            spec[sig, :, lanes] = dot(tf[...], turned[:, lanes]).astype(BF)
            return 0
        lax.fori_loop(0, 4, body, 0)

    def inverse(first, second, conj, sig, at_once):
        def body(n, _):
            lanes = chunk(n)
            ar = spec[first, 0:256, lanes].astype(F32)
            ai = spec[first, 256:512, lanes].astype(F32)
            br = spec[second, 0:256, lanes].astype(F32)
            bi = spec[second, 256:512, lanes].astype(F32)
            if conj:
                pr, pi = ar * br + ai * bi, ar * bi - ai * br
            else:
                pr, pi = ar * br - ai * bi, ar * bi + ai * br
            p = jnp.concatenate([pr.astype(BF), pi.astype(BF)], 0)
            v = dot(ti[...], p)
            vr, vi = v[:256], v[256:]
            c, s = twc[:, lanes], tws[:, lanes]
            wide[:, lanes] = (vr * c - vi * s).astype(BF)
            wide[:, pl.ds(pl.multiple_of(1024 + n * 256, 256), 256)] = (vi * c + vr * s).astype(BF)
            return 0
        lax.fori_loop(0, 4, body, 0)
        deliver(
            sig, sig, ALL,
            lambda lanes: (dot(wide[...], ki[:, lanes]) * (1.0 / LEN)).astype(BF), at_once,
        )

    def upstream(p, lo=0, hi=8):
        flip = p > 0
        h = (1 - hh) if flip else hh
        b0, nb = PASSES[p]
        na = 256 // nb if nb < 256 else 1
        rows = pl.ds(b0, nb)

        def body(t, _):
            at = pl.ds(t * na, na)
            acc = up[at, rows, :].reshape(na * nb, 128) if flip else jnp.zeros((na * nb, 128), F32)
            for y in range(4):
                g = y * 2 + h
                x = jnp.concatenate(
                    [G[4 * g + k, at, rows, :].reshape(na * nb, 128) for k in range(4)], 1
                )
                acc = acc + dot(x, wt[g])
            up[at, rows, :] = acc.reshape(na, nb, 128)
            return 0
        lax.fori_loop(lo // na, hi // na, body, 0)

    def gate(p, slot, at_once):
        b0, nb = PASSES[p]
        rows = pl.ds(b0, nb)
        for a in range(8):
            cat[rows, a * 128:(a + 1) * 128] = (up[a, rows] * qkv[0, a, rows].astype(F32)).astype(BF)
        spread(2, slot, rows, at_once)

    def move(src, dst, k, to):
        pltpu.make_async_remote_copy(
            src_ref=src, dst_ref=dst, send_sem=rs.at[k], recv_sem=rr.at[k],
            device_id=(me, to), device_id_type=MESH,
        ).start()

    def half_part(r, b):
        g = jnp.concatenate(
            [G[4 * r + k, :, b:b + 128, :].reshape(1024, 128) for k in range(4)], 1
        )
        o = jnp.concatenate([out_t[:, a * 256 + b:a * 256 + b + 128] for a in range(8)], 1)
        return dot(o, g)

    def part_first():
        def body(y, _):
            psf[y] = half_part(2 * y + 1 - hh, 0)
            return 0
        lax.fori_loop(0, 4, body, 0)

    def part(flip):
        h = (1 - hh) if flip else hh

        def body(y, _):
            r = 2 * y + h
            if flip:
                z = psf[y] + half_part(r, 128)
            else:
                g = jnp.concatenate([G[4 * r + k].reshape(2048, 128) for k in range(4)], 1)
                z = dot(out_t[...], g)
            ps[r] = (z * (1.0 / math.sqrt(LEN))).astype(BF)
            return 0
        lax.fori_loop(0, 4, body, 0)

        @pl.when(core != h)
        def _():
            for r in (2, 1, 3, 0):
                move(ps.at[2 * chip(r) + h], pr1.at[r], r, sib)

    def combine(flip):
        h = (1 - hh) if flip else hh

        @pl.when(core == h)
        def _():
            for r in (2, 1, 3):
                arrived(pr1.at[r], rr.at[r])
                n = 2 * chip(r) + h
                ps2[r] = (ps[n].astype(F32) + pr1[r].astype(F32)).astype(BF)
                move(ps2.at[r], pr2.at[r], 3 + r, n)

    def weights_go(s):
        if s == 0:
            remote(W.at[ctx], W.at[ctx], ws.at[4], wr.at[4], (me, sib))
            for r in (2, 1, 3):
                todo.append(functools.partial(
                    remote, W.at[ctx], W.at[ctx], ws.at[r], wr.at[r], (me, 2 * chip(r) + core)
                ))
        if s == 2:
            for r in range(1, 4):
                frm = 2 * chip(-r) + core
                arrived(W.at[frm], wr.at[r])
                remote(W.at[frm], W.at[frm], ws.at[4 + r], wr.at[4 + r], (me, sib))

    def weights_in():
        arrived(W.at[sib], wr.at[4])
        for r in range(1, 4):
            arrived(W.at[2 * chip(-r) + 1 - core], wr.at[4 + r])

        def body(g, _):
            wt[g] = W[g].T
            return 0
        lax.fori_loop(0, CTX, body, 0)

    def use_conv(a, z):
        conv[a] = z.astype(BF)

    def turn(a, _):
        o = (qkv[0, a].astype(F32) * conv[a].astype(F32)).astype(BF)
        out_t[:, chunk(a)] = o.T
        return 0

    _, rows0, rows1, rows2 = (pl.ds(*q) for q in PASSES)

    loads["g"].wait()
    e0(0)
    swap(1)
    swap(2)
    swap(3)
    loads["qkv"].wait()
    loads["perm"].wait()
    for a in range(8):
        cat[:, a * 128:(a + 1) * 128] = (qkv[1, a].astype(F32) * qkv[2, a].astype(F32)).astype(BF)
    spread(0, 0, ALL)
    loads["tap"].wait()
    for a in range(8):
        cat[:, a * 128:(a + 1) * 128] = tap[a]
    spread(1, 1, ALL)
    loads["w"].wait()
    weights_go(0)
    e1(0)
    e2(0)
    e3(0, (0,))
    for k in ("kf", "tf", "twc", "tws", "ki", "ti"):
        loads[k].wait()
    e3(0, (-1, 1))
    e3(0, (2,))
    flush()
    swapped(1)
    e0(1)
    e4(0)
    exchanged(0, 0, ALL)
    first_stage(0, 0, 256)
    second_stage(0)
    e1(1)
    swapped(2)
    e0(2)
    exchanged(1, 1, ALL)
    first_stage(1, 0, 256)
    second_stage(1)
    e2(1)
    inverse(1, 0, False, 3, False)
    e3(1, (0,))
    weights_go(2)
    swapped(3)
    e0(3)
    e1(2)
    e3(1, (-1, 1))
    weights_in()
    upstream(0, 0, 4)
    e3(1, (2,))
    upstream(0, 4, 8)
    flush()
    e2(2)
    e1(3)
    exchanged(3, 3, ALL)
    collect(3, use_conv)
    lax.fori_loop(0, 8, turn, 0)
    part(0)
    combine(0)
    e4(1)
    upstream(1)
    gate(1, 2, False)
    e3(2)
    e2(3)
    flush()
    e4(2)
    upstream(2)
    gate(2, 6, False)
    e3(3)
    flush()
    part_first()
    exchanged(2, 2, rows0)
    first_stage(2, *PASSES[1])
    e4(3)
    upstream(3)
    gate(3, 7, True)
    part(1)
    combine(1)
    exchanged(2, 6, rows1)
    first_stage(2, *PASSES[2])

    exchanged(2, 7, rows2)
    first_stage(2, *PASSES[3])
    second_stage(2)
    early = list(sent)
    inverse(0, 2, True, 4, True)
    inverse(1, 2, True, 5, True)

    for a in range(8):
        outs[0, a] = (up[a] * conv[a].astype(F32)).astype(BF)
    writes = [pltpu.make_async_copy(outs.at[0], o_streams.at[0], osem.at[0])]
    writes[-1].start()

    arrived(pr1.at[0], rr.at[0])
    total = ps[ctx].astype(F32) + pr1[0].astype(F32)
    for r in range(1, 4):
        arrived(pr2.at[r], rr.at[3 + r])
        total = total + pr2[r].astype(F32)
    outw[...] = total
    writes.append(pltpu.make_async_copy(outw, o_weight, osem.at[1]))
    writes[-1].start()

    for copy in early:
        copy.wait_send()
    exchanged(4, 4, ALL)

    def use_taps(a, z):
        outs[1, a] = z.astype(BF)
    collect(4, use_taps)
    writes.append(pltpu.make_async_copy(outs.at[1], o_streams.at[1], osem.at[2]))
    writes[-1].start()

    exchanged(5, 5, ALL)

    gathered(5, ALL)
    for n in range(4):
        z = dot(cat[...], perm[:, n * 256:(n + 1) * 256]).astype(BF)
        outs[2, 2 * n] = z[:, :128]
        outs[2, 2 * n + 1] = z[:, 128:]
        pair = pl.ds(2 * n, 2)
        writes.append(pltpu.make_async_copy(outs.at[2, pair], o_streams.at[2, pair], osem.at[3 + n]))
        writes[-1].start()

    for copy in sent[len(early):]:
        copy.wait_send()
    for k in range(7):
        pltpu.make_async_remote_copy(
            src_ref=ps.at[0], dst_ref=pr1.at[0], send_sem=rs.at[k], recv_sem=rr.at[k],
            device_id=(me, sib), device_id_type=MESH,
        ).wait_send()
    for copy in writes:
        copy.wait()


def finish(found, key, value, weights, o_streams, o_filter, o_weight):
    o_streams[0] = found[0]
    o_filter[...] = found[1].astype(F32) * (1.0 / math.sqrt(LEN))
    mix = found[2].astype(F32)
    o_streams[1] = (mix * value[0].astype(F32)).astype(BF)
    o_streams[2] = (mix * key[0].astype(F32)).astype(BF)
    o_weight[...] = weights[...]


def shards(projected, filter_taps, out_grad, out_weight):
    consts = [jnp.asarray(t) for t in tables()]
    vm = pltpu.VMEM
    sem = pltpu.SemaphoreType.DMA
    found, weights = pl.pallas_call(
        kernel,
        out_shape=(
            jax.ShapeDtypeStruct((3, 8, 256, 128), BF),
            jax.ShapeDtypeStruct((128, 512), F32),
        ),
        in_specs=[pl.BlockSpec(memory_space=pl.ANY)] * 11,
        out_specs=(pl.BlockSpec(memory_space=pl.ANY),) * 2,
        scratch_shapes=[
            vm((3, 8, 256, 128), BF),
            vm((8, 256, 128), BF),
            vm((32, 8, 256, 128), BF),
            vm((8, 128, 512), BF),
            vm((8, 512, 128), BF),
            vm((1024, 1024), BF),
            vm((1024, 2048), BF),
            vm((2048, 1024), BF),
            vm((512, 512), BF),
            vm((512, 512), BF),
            vm((256, 1024), F32),
            vm((256, 1024), F32),
            vm((256, 1024), BF),
            vm((6, 8, 256, 128), BF),
            vm((6, 8, 256, 128), BF),
            vm((3, 512, 1024), BF),
            vm((512, 1024), BF),
            vm((256, 2048), BF),
            vm((8, 256, 128), F32),
            vm((8, 256, 128), BF),
            vm((128, 2048), BF),
            vm((8, 128, 512), BF),
            vm((4, 128, 512), F32),
            vm((4, 128, 512), BF),
            vm((4, 128, 512), BF),
            vm((4, 128, 512), BF),
            vm((3, 8, 256, 128), BF),
            vm((128, 512), F32),
            sem((11,)), sem((7,)),
            sem((184,)), sem((32, 12)),
            sem((8, 8)), sem((8, 8)),
            sem((13,)), sem((8,)),
            sem((8,)), sem((8,)),
        ],
        compiler_params=pltpu.CompilerParams(
            collective_id=0, has_side_effects=True, vmem_limit_bytes=60 * 2**20
        ),
    )(
        projected.reshape(3, 8, 256, 128), filter_taps.reshape(8, 256, 128),
        out_grad.reshape(8, 256, 128), out_weight, *consts,
    )
    rows = pl.BlockSpec((3, 1024, 128), lambda i: (0, i, 0))
    keys = pl.BlockSpec((1, 1024, 128), lambda i: (1, i, 0))
    values = pl.BlockSpec((1, 1024, 128), lambda i: (2, i, 0))
    part = pl.BlockSpec((64, 512), lambda i: (i, 0))
    return pl.pallas_call(
        finish,
        grid=(2,),
        out_shape=(
            jax.ShapeDtypeStruct((3, 2048, 128), BF),
            jax.ShapeDtypeStruct((2048, 128), F32),
            jax.ShapeDtypeStruct((128, 512), F32),
        ),
        in_specs=[rows, keys, values, part],
        out_specs=(rows, pl.BlockSpec((1024, 128), lambda i: (i, 0)), part),
    )(found.reshape(3, 2048, 128), projected, projected, weights)


def solution(mesh):
    placed = (P(None, "context", "dp"), P("context", "dp"), P("context", "dp"), P("dp", "context"))
    return jax.shard_map(
        shards,
        mesh=mesh,
        in_specs=placed,
        out_specs=(P(None, "context", "dp"), P("context", "dp"), P("dp", "context")),
        check_vma=False,
    )
```
